512 devices in a mesh: dp: 16 (over y_hi, x, core), expert: 32 (over z, y_lo).
Axes of the slice: x: 4, y: 4 (y_hi: 2, y_lo: 2; y = y_hi * 2 + y_lo), z: 16, core: 2. Of those that a mesh axis runs over, the one named last changes fastest.
Arguments:
- grad_rows: bfloat16 [16, 256, 16, 3584], P('dp', 'expert'), may hold values from -6 to 6
- router_weight: float32 [16, 256, 16], P('dp', 'expert'), may hold values from 0.05 to 0.6
- send_counts: int32 [16, 256], P('dp', 'expert'), may hold values from 1 to 16, as said below
- gate_stash: bfloat16 [16, 512, 8192], P('dp', None, 'expert'), may hold values from -6 to 6
- up_stash: bfloat16 [16, 512, 8192], P('dp', None, 'expert'), may hold values from -6 to 6
- master_weight: float32 [3584, 8192], P('dp', 'expert'), may hold values from -0.1875 to 0.1875
- first_moment: float32 [3584, 8192], P('dp', 'expert'), may hold values from -18 to 18
- second_moment: float32 [3584, 8192], P('dp', 'expert'), may hold values from 10 to 100
Outputs:
- d_gate: bfloat16 [16, 512, 8192], P('dp', None, 'expert')
- d_up: bfloat16 [16, 512, 8192], P('dp', None, 'expert')
- new_master: float32 [3584, 8192], P('dp', 'expert')
- new_first: float32 [3584, 8192], P('dp', 'expert')
- new_second: float32 [3584, 8192], P('dp', 'expert')
- fresh_weight: bfloat16 [3584, 8192], P(None, 'expert')
The draws below stay inside these ranges and needn't reach their ends.
Inputs may be any that keep to these rules, and one draw needn't show every extreme that they name: `send_counts`: in every replica one expert in flight receives exactly 16 rows from every source; the other counts are at most 8.
All inputs are finite; a program needn't handle non-finite values.
Results may differ from the reference program's by a relative error of at most 0.009.
Values may be sent and summed in bfloat16 or wider, within the bound.
A program may use at most 64 MiB of HBM per device.

```python
import math
import jax
import jax.numpy as jnp
from jax import lax

D_W = 3584
FF = 1024
SLOT = 16
FLIGHT = 8
N_DP = 16
N_EXPERT = 32


def draw_send_counts(key, part):
    key = jax.random.fold_in(key, 7)
    base = jax.random.randint(jax.random.fold_in(key, 1), (N_DP, N_EXPERT, FLIGHT), 1, SLOT // 2 + 1)
    hottest = jax.random.randint(jax.random.fold_in(key, 2), (N_DP, 1, 1), 0, FLIGHT)
    experts = jnp.arange(FLIGHT, dtype=jnp.int32)[None, None, :]
    counts = jnp.where(experts == hottest, SLOT, base)
    return counts.reshape(N_DP, N_EXPERT * FLIGHT).astype(jnp.int32)


def steps_of(own_key, dims, pieces, smallest, largest):
    def one(axis_at, parts):
        heights = jax.random.uniform(jax.random.fold_in(jax.random.fold_in(own_key, 6), axis_at), (parts,), jnp.float32, smallest / len(pieces), largest / len(pieces))
        return jnp.repeat(jnp.exp(heights), dims[axis_at] // parts).reshape((-1,) + (1,) * (len(dims) - axis_at - 1))

    loudness = one(*pieces[0])
    for cut in pieces[1:]:
        loudness = loudness * one(*cut)
    return loudness


def centred(key, dims, scale, most, pieces=(), kind=jnp.bfloat16):
    gain = steps_of(key, dims, pieces, -0.22, 0.18) if pieces else 1.0
    drawn = jax.random.normal(key, dims, jnp.float32) * scale * gain
    return jnp.minimum(jnp.maximum(drawn, -most), most).astype(kind)


def setup_inputs(seed: int = 0) -> dict:
    key_of = jax.random.split(jax.random.key(seed), 9)
    return {
        "grad_rows": centred(key_of[0], (N_DP, N_EXPERT * FLIGHT, SLOT, D_W), 1.0, 6.0, ((0, 16), (1, 32))),
        "router_weight": jnp.clip(jnp.exp(math.log(0.6) - 2.4849067 * jax.random.uniform(key_of[1], (N_DP, N_EXPERT * FLIGHT, SLOT), jnp.float32) ** steps_of(key_of[1], (N_DP, N_EXPERT * FLIGHT, SLOT), ((0, 16), (1, 32)), -0.2, 0.2)), 0.05, 0.6),
        "send_counts": draw_send_counts(jax.random.fold_in(key_of[8], 71), 0),
        "gate_stash": centred(key_of[3], (N_DP, N_EXPERT * SLOT, FLIGHT * FF), 1.0, 6.0, ((0, 16), (2, 32))),
        "up_stash": centred(key_of[4], (N_DP, N_EXPERT * SLOT, FLIGHT * FF), 1.0, 6.0, ((0, 16), (2, 32))),
        "master_weight": centred(key_of[5], (D_W, FLIGHT * FF), FF ** -0.5, 0.1875, ((0, 16), (1, 32)), jnp.float32),
        "first_moment": centred(key_of[6], (D_W, FLIGHT * FF), 3.0, 18.0, ((0, 16), (1, 32)), jnp.float32),
        "second_moment": jnp.clip(jnp.exp(math.log(100.0) - 2.3025851 * jax.random.uniform(key_of[7], (D_W, FLIGHT * FF), jnp.float32) ** steps_of(key_of[7], (D_W, FLIGHT * FF), ((0, 16), (1, 32)), -0.2, 0.2)), 10.0, 100.0),
    }


learning_rate = 0.01
beta_one = 0.9
beta_two = 0.95
decay_rate = 0.1
epsilon = 1e-08

def reference(grad_rows, router_weight, send_counts, gate_stash, up_stash, master_weight, first_moment, second_moment):
    flight = master_weight.shape[1] // FF
    grads = grad_rows.reshape(N_DP, N_EXPERT, flight, SLOT, D_W)
    probs = router_weight.reshape(N_DP, N_EXPERT, flight, SLOT)
    counts = send_counts.reshape(N_DP, N_EXPERT, flight)
    slots = jnp.arange(SLOT, dtype=jnp.int32)

    def one_expert(which):
        which = which.astype(jnp.int32)
        rows_in = lax.dynamic_index_in_dim(grads, which, 2, keepdims=False)
        weights = lax.dynamic_index_in_dim(probs, which, 2, keepdims=False)
        limit = lax.dynamic_index_in_dim(counts, which, 2, keepdims=False)
        live = slots[None, None, :] < limit[:, :, None]
        scaled = jnp.where(live[..., None], weights[..., None] * rows_in.astype(jnp.float32), jnp.float32(0.0))
        scaled = scaled.astype(jnp.bfloat16).reshape(N_DP * N_EXPERT * SLOT, D_W)
        start = (which * FF).astype(jnp.int32)
        gate = lax.dynamic_slice_in_dim(gate_stash, start, FF, 2).astype(jnp.float32).reshape(-1, FF)
        up = lax.dynamic_slice_in_dim(up_stash, start, FF, 2).astype(jnp.float32).reshape(-1, FF)
        sigmoid_gate = jax.nn.sigmoid(gate)
        activated = gate * sigmoid_gate
        hidden = (activated * up).astype(jnp.bfloat16)
        gradient = lax.dot_general(scaled, hidden, (((0,), (0,)), ((), ())), preferred_element_type=jnp.float32)
        master = lax.dynamic_slice_in_dim(master_weight, start, FF, 1)
        moment_a = lax.dynamic_slice_in_dim(first_moment, start, FF, 1)
        moment_b = lax.dynamic_slice_in_dim(second_moment, start, FF, 1)
        current = master.astype(jnp.bfloat16)
        d_hidden = jnp.dot(scaled, current, preferred_element_type=jnp.float32)
        grad_gate = (d_hidden * up * sigmoid_gate * (1.0 + gate * (1.0 - sigmoid_gate))).astype(jnp.bfloat16)
        grad_up = (d_hidden * activated).astype(jnp.bfloat16)
        moment_a = beta_one * moment_a + (1.0 - beta_one) * gradient
        moment_b = beta_two * moment_b + (1.0 - beta_two) * gradient * gradient
        step_size = moment_a / (1.0 - beta_one ** 5) / (jnp.sqrt(moment_b / (1.0 - beta_two ** 5)) + epsilon)
        master = master - learning_rate * (step_size + decay_rate * master)
        return (grad_gate.reshape(N_DP, N_EXPERT * SLOT, FF), grad_up.reshape(N_DP, N_EXPERT * SLOT, FF), master, moment_a, moment_b, master.astype(jnp.bfloat16))
    outs = lax.map(one_expert, jnp.arange(flight, dtype=jnp.int32))

    def rows_layout(stacked):
        return stacked.transpose(1, 2, 0, 3).reshape(N_DP, N_EXPERT * SLOT, flight * FF)

    def weight_layout(stacked):
        return stacked.transpose(1, 0, 2).reshape(D_W, flight * FF)
    return (rows_layout(outs[0]), rows_layout(outs[1]), weight_layout(outs[2]), weight_layout(outs[3]), weight_layout(outs[4]), weight_layout(outs[5]))
```

```python
import functools

import jax
import jax.numpy as jnp
from jax import lax
from jax.experimental import pallas as pl
from jax.experimental.pallas import tpu as pltpu
from jax.sharding import PartitionSpec as P

UNITS = (2, 2, 2, 1)
STRIP = 32

learning_rate = 0.01
beta_one = 0.9
beta_two = 0.95
decay_rate = 0.1
epsilon = 1e-08

MESH = pl.DeviceIdType.MESH
BF16 = jnp.bfloat16
F32 = jnp.float32


def kernel(
    nx,
    nz,
    rows_ref,
    weight_ref,
    count_ref,
    gate_ref,
    up_ref,
    master_ref,
    first_ref,
    second_ref,
    dgate_ref,
    dup_ref,
    newm_ref,
    newf_ref,
    news_ref,
    fresh_ref,
    *scratch,
):
    chunks = len(UNITS)
    send, recv, part, gsend, grecv, summed, pieces = (
        scratch[k * chunks : (k + 1) * chunks] for k in range(7)
    )
    (
        wown,
        wfull,
        hid,
        total,
        dh_out,
        dh_in,
        send_s,
        recv_s,
        pass_s,
        ws_s,
        wr_s,
        wcs_s,
        wcr_s,
        pair_s,
        gs_s,
        gr_s,
        ps_s,
        pr_s,
        as_s,
        ar_s,
        cs_s,
        cr_s,
    ) = scratch[7 * chunks :]
    flight, slots, width = rows_ref.shape
    shard, cols = master_ref.shape
    half = width // 2
    near = nz // 2

    i, ez = lax.axis_index("dp"), lax.axis_index("expert")
    c, x, yh = lax.rem(i, 2), lax.rem(lax.div(i, 2), nx), lax.div(i, 2 * nx)
    z, yl = lax.div(ez, 2), lax.rem(ez, 2)
    zl = lax.rem(z, 2)
    sibling = {"dp": i + 1 - 2 * c}
    z_pair = {"expert": ez + 2 - 4 * zl}
    y_pair = {"expert": ez + 1 - 2 * yl}

    def dp_of(yh_, x_):
        return yh_ * (2 * nx) + x_ * 2 + c

    def remote(src, dst, s, r, to):
        return pltpu.make_async_remote_copy(
            src_ref=src, dst_ref=dst, send_sem=s, recv_sem=r, device_id=to, device_id_type=MESH
        )

    def source_z(zz, zzl, t):
        return lax.rem(zz + jnp.where(zzl == 0, nz - t, t), nz)

    barrier = pltpu.get_barrier_semaphore()

    def greet(to):
        pl.semaphore_signal(barrier, inc=1, device_id=to, device_id_type=MESH)

    greet(sibling)
    greet(z_pair)

    def greet_line(t, carry):
        zs = source_z(z, zl, t)
        for ys in range(2):

            @pl.when(jnp.logical_or(t != 0, yl != ys))
            def _():
                greet({"expert": zs * 2 + ys})

        return carry

    lax.fori_loop(0, near, greet_line, 0)

    def greet_plane(k, carry):
        yh_, x_ = lax.div(k, nx), lax.rem(k, nx)
        for ys in range(2):

            @pl.when(jnp.logical_or(dp_of(yh_, x_) != i, yl != ys))
            def _():
                greet({"dp": dp_of(yh_, x_), "expert": z * 2 + ys})

        return carry

    lax.fori_loop(0, 2 * nx, greet_plane, 0)

    lane = lax.broadcasted_iota(jnp.int32, (slots, 128), 1)
    group = lax.div(lane, STRIP)
    eye = lax.broadcasted_iota(jnp.int32, (slots, slots), 0) == lax.broadcasted_iota(
        jnp.int32, (slots, slots), 1
    )
    slot_of = lax.broadcasted_iota(jnp.int32, (slots, 1), 0)
    per_tile = 128 // STRIP

    def scale(e, carry):
        row = weight_ref[pl.ds(e, 1), :]
        factor = jnp.sum(
            jnp.where(eye, jnp.broadcast_to(row, (slots, slots)), 0.0), axis=1, keepdims=True
        )
        factor = jnp.where(slot_of < count_ref[0, e], factor, 0.0)
        scaled = rows_ref[e].astype(F32) * factor
        for h in range(2):
            start = 0
            for m, units in enumerate(UNITS):
                span = 2 * nx * units * STRIP
                for tile in range(span // 128):
                    out = None
                    for a in range(per_tile):
                        owner, strip = divmod(tile * per_tile + a, units)
                        at = h * half + owner * shard + (start + strip) * STRIP
                        base, off = at // 128 * 128, at % 128
                        moved = scaled[:, base : base + 128]
                        shift = (a * STRIP - off) % 128
                        if shift:
                            moved = pltpu.roll(moved, shift, 1)
                        out = moved if out is None else jnp.where(group == a, moved, out)
                    send[m][e, h, :, tile * 128 : (tile + 1) * 128] = out.astype(BF16)
                start += units
        return carry

    lax.fori_loop(0, flight, scale, 0)
    wown[...] = master_ref[...].astype(BF16)

    pl.semaphore_wait(barrier, 2 * near - 1 + 4 * nx - 1 + 2)

    def exchange(m):
        def one(k, carry):
            t = near - 1 - k
            up_way = lax.rem(z + t, 2) == 0
            zd = lax.rem(z + jnp.where(up_way, t, nz - t), nz)
            e = lax.div(zd, 2)
            for h in range(2):
                own = jnp.logical_and(t == 0, yl == h)

                @pl.when(jnp.logical_not(own))
                def _():
                    remote(
                        send[m].at[e, h],
                        recv[m].at[ez],
                        send_s.at[m, t, h],
                        recv_s.at[m, ez],
                        {"expert": zd * 2 + h},
                    ).start()

                @pl.when(own)
                def _():
                    pltpu.make_async_copy(
                        send[m].at[e, h], recv[m].at[ez], recv_s.at[m, ez]
                    ).start()

            return carry

        lax.fori_loop(0, near, one, 0)

    exchange(0)

    def spread_weights(k, carry):
        yh_, x_ = lax.div(k, nx), lax.rem(k, nx)
        to = dp_of(yh_, x_)
        slot = wfull.at[yl, x, c]
        own = jnp.logical_and(to == i, yl == yh)

        @pl.when(jnp.logical_not(own))
        def _():
            remote(
                wown, slot, ws_s.at[yh_, x_], wr_s.at[yl, x], {"dp": to, "expert": z * 2 + yh}
            ).start()

        @pl.when(own)
        def _():
            pltpu.make_async_copy(wown, slot, wr_s.at[yl, x]).start()

        return carry

    lax.fori_loop(0, 2 * nx, spread_weights, 0)
    for m in range(1, chunks):
        exchange(m)

    def swish(k, carry):
        at = pl.ds(pl.multiple_of(k * 128, 128), 128)
        gate = gate_ref[at, :].astype(F32)
        up = up_ref[at, :].astype(F32)
        hid[yl, at, :] = (gate * jax.nn.sigmoid(gate) * up).astype(BF16)
        return carry

    lax.fori_loop(0, gate_ref.shape[0] // 128, swish, 0)
    hid_copy = remote(hid.at[yl], hid.at[yl], pair_s.at[0], pair_s.at[1], y_pair)
    hid_copy.start()

    def pass_on(m):
        def one(k, carry):
            t = near - 1 - k
            for ys in range(2):
                s = source_z(z, zl, t) * 2 + ys
                copy = remote(
                    recv[m].at[s], recv[m].at[s], pass_s.at[m, t, ys], recv_s.at[m, s], z_pair
                )
                copy.wait_recv()
                copy.start()
            return carry

        lax.fori_loop(0, near, one, 0)

    def arrived(m):
        def one(k, carry):
            t = near - 1 - k
            for ys in range(2):
                s = source_z(z + 1 - 2 * zl, 1 - zl, t) * 2 + ys
                remote(
                    recv[m].at[s], recv[m].at[s], pass_s.at[m, t, ys], recv_s.at[m, s], z_pair
                ).wait_recv()
            return carry

        lax.fori_loop(0, near, one, 0)

    def weight_copy(k):
        yl_, x_ = lax.div(k, nx), lax.rem(k, nx)
        return yl_, x_, remote(
            wfull.at[yl_, x_, c],
            wfull.at[yl_, x_, c],
            wcs_s.at[yl_, x_],
            wcr_s.at[yl_, x_],
            sibling,
        )

    def weights_to_sibling(k, carry):
        yl_, x_, copy = weight_copy(k)
        remote(wown, wfull.at[yl_, x_, c], ws_s.at[0, 0], wr_s.at[yl_, x_], sibling).wait_recv()
        copy.start()
        return carry

    def weights_arrived(k, carry):
        weight_copy(k)[2].wait_recv()
        return carry

    starts = [sum(UNITS[:m]) * STRIP for m in range(chunks)]
    counts = [units * STRIP for units in UNITS]

    def to_sibling(m):
        return remote(gsend[m], grecv[m], gs_s.at[m], gr_s.at[m], sibling)

    def columns_of(m):
        return recv[m][...].reshape(recv[m].shape[0] * slots, recv[m].shape[2])

    def gradient(m):
        for y_ in range(2):
            part[m][y_] = lax.dot_general(
                columns_of(m), hid[y_], (((0,), (0,)), ((), ())), preferred_element_type=F32
            ).reshape(nx, 2, counts[m], cols)
        gsend[m][...] = part[m][:, :, 1 - c].astype(BF16)
        to_sibling(m).start()

    def back(m):
        for y_ in range(2):
            block = wfull[y_, :, :, starts[m] : starts[m] + counts[m], :].reshape(-1, cols)
            product = jnp.dot(columns_of(m), block, preferred_element_type=F32)
            if m:
                total[y_] += product
            else:
                total[y_] = product

    def piece_copy(m, k):
        y_, x_ = lax.div(k, nx), lax.rem(k, nx)
        to = dp_of(yl, x_)
        own = jnp.logical_and(to == i, yl == y_)
        src, dst, sem = summed[m].at[y_, x_], pieces[m].at[yh * nx + x], pr_s.at[m, yh * nx + x]
        return (
            own,
            remote(src, dst, ps_s.at[m, k], sem, {"dp": to, "expert": z * 2 + y_}),
            (src, dst, sem),
        )

    def reduce_pieces(m):
        to_sibling(m).wait_recv()
        summed[m][...] = (part[m][:, :, c] + grecv[m][...].astype(F32)).astype(BF16)

        def one(k, carry):
            own, copy, local = piece_copy(m, k)

            @pl.when(jnp.logical_not(own))
            def _():
                copy.start()

            @pl.when(own)
            def _():
                pltpu.make_async_copy(*local).start()

            return carry

        lax.fori_loop(0, 2 * nx, one, 0)

    def fresh_slot(m, k, core):
        return fresh_ref.at[k, core, starts[m] : starts[m] + counts[m]]

    def fresh_copy(m, k, source):
        return remote(
            fresh_slot(m, source, c),
            fresh_slot(m, source, c),
            as_s.at[m, k],
            ar_s.at[m, source],
            {"dp": k * 2 + c},
        )

    def update(m):
        def one(k, carry):
            remote(
                summed[m].at[0, 0], pieces[m].at[k], ps_s.at[m, k], pr_s.at[m, k], sibling
            ).wait_recv()
            return carry

        lax.fori_loop(0, 2 * nx, one, 0)
        at = slice(starts[m], starts[m] + counts[m])
        grad = jnp.sum(pieces[m][...].astype(F32), axis=0)
        master = master_ref[at, :]
        moment_a = beta_one * first_ref[at, :] + (1.0 - beta_one) * grad
        moment_b = beta_two * second_ref[at, :] + (1.0 - beta_two) * grad * grad
        step = (
            moment_a
            / (1.0 - beta_one**5)
            / (jnp.sqrt(moment_b / (1.0 - beta_two**5)) + epsilon)
        )
        updated = master - learning_rate * (step + decay_rate * master)
        newm_ref[at, :] = updated
        newf_ref[at, :] = moment_a
        news_ref[at, :] = moment_b
        me = yh * nx + x
        fresh_ref[me, c, at, :] = updated.astype(BF16)

        def send_one(k, carry):
            @pl.when(k != me)
            def _():
                fresh_copy(m, k, me).start()

            return carry

        lax.fori_loop(0, 2 * nx, send_one, 0)

    def fresh_to_sibling(m):
        at = pl.ds(starts[m], counts[m])
        return remote(
            fresh_ref.at[:, c, at], fresh_ref.at[:, c, at], cs_s.at[m], cr_s.at[m], sibling
        )

    def gather(m):
        me = yh * nx + x

        def one(k, carry):
            @pl.when(k != me)
            def _():
                fresh_copy(m, k, k).wait_recv()

            return carry

        lax.fori_loop(0, 2 * nx, one, 0)
        fresh_to_sibling(m).start()

    dh_copy = remote(dh_out, dh_in, pair_s.at[2], pair_s.at[3], y_pair)

    def finish_hidden():
        dh_copy.wait_recv()

        def one(k, carry):
            at = pl.ds(pl.multiple_of(k * 128, 128), 128)
            gate = gate_ref[at, :].astype(F32)
            up = up_ref[at, :].astype(F32)
            sig = jax.nn.sigmoid(gate)
            dh = total[yl, at, :] + dh_in[at, :].astype(F32)
            dgate_ref[at, :] = (dh * up * sig * (1.0 + gate * (1.0 - sig))).astype(BF16)
            dup_ref[at, :] = (dh * (gate * sig)).astype(BF16)
            return carry

        lax.fori_loop(0, gate_ref.shape[0] // 128, one, 0)

    pass_on(0)
    lax.fori_loop(0, 2 * nx, weights_to_sibling, 0)
    if chunks > 1:
        pass_on(1)
    hid_copy.wait_recv()
    for m in range(chunks):
        arrived(m)
        gradient(m)
        if m == 0:
            lax.fori_loop(0, 2 * nx, weights_arrived, 0)
        back(m)
        if m == chunks - 1:
            dh_out[...] = total[1 - yl].astype(BF16)
            dh_copy.start()
        reduce_pieces(m)
        if m >= 1:
            update(m - 1)
        if m + 2 < chunks:
            pass_on(m + 2)
        if m >= 2:
            gather(m - 2)
    update(chunks - 1)
    if chunks > 1:
        gather(chunks - 2)
    finish_hidden()
    gather(chunks - 1)

    for m in range(chunks):
        fresh_to_sibling(m).wait()
        to_sibling(m).wait_send()

        def sent(t, carry, m=m):
            for h in range(2):

                @pl.when(jnp.logical_or(t != 0, yl != h))
                def _():
                    remote(
                        send[m].at[0, h],
                        recv[m].at[0],
                        send_s.at[m, t, h],
                        recv_s.at[m, 0],
                        z_pair,
                    ).wait_send()

                remote(
                    recv[m].at[0], recv[m].at[0], pass_s.at[m, t, h], recv_s.at[m, 0], z_pair
                ).wait_send()
            return carry

        lax.fori_loop(0, near, sent, 0)

        def sent_plane(k, carry, m=m):
            own, copy, _ = piece_copy(m, k)

            @pl.when(jnp.logical_not(own))
            def _():
                copy.wait_send()

            @pl.when(k != yh * nx + x)
            def _():
                fresh_copy(m, k, k).wait_send()

            return carry

        lax.fori_loop(0, 2 * nx, sent_plane, 0)

    def sent_weights(k, carry):
        yh_, x_ = lax.div(k, nx), lax.rem(k, nx)

        @pl.when(jnp.logical_not(jnp.logical_and(dp_of(yh_, x_) == i, yl == yh)))
        def _():
            remote(
                wown, wfull.at[0, 0, 0], ws_s.at[yh_, x_], wr_s.at[0, 0], sibling
            ).wait_send()

        weight_copy(k)[2].wait_send()
        return carry

    lax.fori_loop(0, 2 * nx, sent_weights, 0)
    hid_copy.wait_send()
    dh_copy.wait_send()


def local(nx, nz, rows, weight, count, gate, up, master, first, second):
    _, flight, slots, width = rows.shape
    shard, cols = master.shape
    _, received, _ = gate.shape
    chunks = len(UNITS)
    counts = [units * STRIP for units in UNITS]
    assert sum(counts) == shard and cols % 128 == 0
    spans = [2 * nx * n for n in counts]
    vmem = pl.BlockSpec(memory_space=pltpu.VMEM)
    dma = pltpu.SemaphoreType.DMA
    near = nz // 2
    scratch = (
        [pltpu.VMEM((flight, 2, slots, n), BF16) for n in spans]
        + [pltpu.VMEM((2 * nz, slots, n), BF16) for n in spans]
        + [pltpu.VMEM((2, nx, 2, n, cols), F32) for n in counts]
        + [pltpu.VMEM((2, nx, n, cols), BF16) for n in counts]
        + [pltpu.VMEM((2, nx, n, cols), BF16) for n in counts]
        + [pltpu.VMEM((2, nx, n, cols), BF16) for n in counts]
        + [pltpu.VMEM((2 * nx, n, cols), BF16) for n in counts]
        + [
            pltpu.VMEM((shard, cols), BF16),
            pltpu.VMEM((2, nx, 2, shard, cols), BF16),
            pltpu.VMEM((2, received, cols), BF16),
            pltpu.VMEM((2, received, cols), F32),
            pltpu.VMEM((received, cols), BF16),
            pltpu.VMEM((received, cols), BF16),
            dma((chunks, near, 2)),
            dma((chunks, 2 * nz)),
            dma((chunks, near, 2)),
            dma((2, nx)),
            dma((2, nx)),
            dma((2, nx)),
            dma((2, nx)),
            dma((4,)),
            dma((chunks,)),
            dma((chunks,)),
            dma((chunks, 2 * nx)),
            dma((chunks, 2 * nx)),
            dma((chunks, 2 * nx)),
            dma((chunks, 2 * nx)),
            dma((chunks,)),
            dma((chunks,)),
        ]
    )
    outs = pl.pallas_call(
        functools.partial(kernel, nx, nz),
        out_shape=[
            jax.ShapeDtypeStruct((received, cols), BF16),
            jax.ShapeDtypeStruct((received, cols), BF16),
            jax.ShapeDtypeStruct((shard, cols), F32),
            jax.ShapeDtypeStruct((shard, cols), F32),
            jax.ShapeDtypeStruct((shard, cols), F32),
            jax.ShapeDtypeStruct((2 * nx, 2, shard, cols), BF16),
        ],
        in_specs=[vmem, vmem, pl.BlockSpec(memory_space=pltpu.SMEM)] + [vmem] * 5,
        out_specs=[vmem] * 6,
        scratch_shapes=scratch,
        compiler_params=pltpu.CompilerParams(
            collective_id=0, has_side_effects=True, vmem_limit_bytes=50 * 1024 * 1024
        ),
    )(rows[0], weight[0], count, gate[0], up[0], master, first, second)
    return (
        outs[0][None],
        outs[1][None],
        outs[2],
        outs[3],
        outs[4],
        outs[5].reshape(4 * nx * shard, cols),
    )


def solution(mesh):
    nx, nz = mesh.shape["dp"] // 4, mesh.shape["expert"] // 2
    placed = (
        P("dp", "expert", None, None),
        P("dp", "expert", None),
        P("dp", "expert"),
        P("dp", None, "expert"),
        P("dp", None, "expert"),
        P("dp", "expert"),
        P("dp", "expert"),
        P("dp", "expert"),
    )
    return jax.shard_map(
        functools.partial(local, nx, nz),
        mesh=mesh,
        in_specs=placed,
        out_specs=(
            P("dp", None, "expert"),
            P("dp", None, "expert"),
            P("dp", "expert"),
            P("dp", "expert"),
            P("dp", "expert"),
            P(None, "expert"),
        ),
        check_vma=False,
    )
```

```python
import functools

import jax
import jax.numpy as jnp
from jax import lax
from jax.experimental import pallas as pl
from jax.experimental.pallas import tpu as pltpu
from jax.sharding import PartitionSpec as P

UNITS = (2, 2, 2, 1)
BEGIN = (0, 0, 0, 0)
STRIP = 32

learning_rate = 0.01
beta_one = 0.9
beta_two = 0.95
decay_rate = 0.1
epsilon = 1e-08

MESH = pl.DeviceIdType.MESH
BF16 = jnp.bfloat16
F32 = jnp.float32


def step_size(near, k):
    return (near - k) // 2 + 2


def step_start(near, k):
    return sum(step_size(near, j) for j in range(1, k))


def kernel(
    nx,
    nz,
    rows_hbm,
    weight_hbm,
    count_hbm,
    gate_hbm,
    up_hbm,
    master_hbm,
    first_hbm,
    second_hbm,
    dgate_ref,
    dup_ref,
    newm_ref,
    newf_ref,
    news_ref,
    fresh_ref,
    *scratch,
):
    chunks = len(UNITS)
    (
        outward,
        halves,
        origin,
        ring,
        last,
        columns,
        part,
        gsend,
        grecv,
        summed,
        across,
        row_sum,
        pieces,
    ) = (scratch[k * chunks : (k + 1) * chunks] for k in range(13))
    (
        rows_ref,
        weight_ref,
        count_ref,
        gate_ref,
        up_ref,
        master_ref,
        first_ref,
        second_ref,
        in_s,
        scaled,
        wown,
        wfull,
        hid,
        total,
        dh_out,
        dh_in,
        ys_s,
        yr_s,
        zs_s,
        zr_s,
        ws_s,
        wr_s,
        pair_s,
        gs_s,
        gr_s,
        xs_s,
        xr_s,
        ps_s,
        pr_s,
        as_s,
        ar_s,
        cs_s,
        cr_s,
    ) = scratch[13 * chunks :]
    flight, slots, width = rows_ref.shape
    shard, cols = master_ref.shape
    half = width // 2
    near = nz // 2
    low = slots // 2

    i, ez = lax.axis_index("dp"), lax.axis_index("expert")
    c, x, yh = lax.rem(i, 2), lax.rem(lax.div(i, 2), nx), lax.div(i, 2 * nx)
    z, yl = lax.div(ez, 2), lax.rem(ez, 2)
    zl, own_expert = lax.rem(z, 2), lax.div(z, 2)
    sibling = {"dp": i + 1 - 2 * c}
    z_pair = {"expert": ez + 2 - 4 * zl}
    y_pair = {"expert": ez + 1 - 2 * yl}
    y_across = {"dp": i + (1 - 2 * yh) * 2 * nx}
    z_next = (
        {"expert": lax.rem(z + 1, nz) * 2 + yl},
        {"expert": lax.rem(z + nz - 1, nz) * 2 + yl},
    )

    def dp_of(yh_, x_):
        return yh_ * (2 * nx) + x_ * 2 + c

    def x_next(step):
        return {"dp": dp_of(yh, lax.rem(x + step, nx))}

    def remote(src, dst, s, r, to):
        return pltpu.make_async_remote_copy(
            src_ref=src, dst_ref=dst, send_sem=s, recv_sem=r, device_id=to, device_id_type=MESH
        )

    loads = [
        pltpu.make_async_copy(src, dst, in_s.at[k])
        for k, (src, dst) in enumerate(
            (
                (rows_hbm, rows_ref),
                (weight_hbm, weight_ref),
                (count_hbm, count_ref),
                (master_hbm, master_ref),
                (gate_hbm, gate_ref),
                (up_hbm, up_ref),
                (first_hbm, first_ref),
                (second_hbm, second_ref),
            )
        )
    ]
    for load in loads:
        load.start()

    barrier = pltpu.get_barrier_semaphore()

    def greet(to):
        pl.semaphore_signal(barrier, inc=1, device_id=to, device_id_type=MESH)

    greet(z_next[0])
    greet(z_next[1])
    greet(sibling)

    greet(y_pair)
    greet(y_across)
    greet({"dp": dp_of(1 - yh, x), "expert": ez + 1 - 2 * yl})
    for step in range(1, nx):
        greet(x_next(step))

    for load in loads[:3]:
        load.wait()
    eye = lax.broadcasted_iota(jnp.int32, (slots, slots), 0) == lax.broadcasted_iota(
        jnp.int32, (slots, slots), 1
    )
    slot_of = lax.broadcasted_iota(jnp.int32, (slots, 1), 0)
    for e in range(flight):
        factor = jnp.sum(
            jnp.where(eye, jnp.broadcast_to(weight_ref[e : e + 1, :], (slots, slots)), 0.0),
            axis=1,
            keepdims=True,
        )
        factor = jnp.where(slot_of < count_ref[:, e : e + 1], factor, 0.0)
        block = rows_ref[e].astype(F32) * factor
        for h in range(2):
            side = block[:, h * half : (h + 1) * half]
            scaled[h, e] = side[:low]
            if e:
                scaled[h, flight] += side[low:]
            else:
                scaled[h, flight] = side[low:]
    expert_of = lax.broadcasted_iota(jnp.int32, (1, flight), 1)
    hot = jnp.max(
        jnp.where(jnp.logical_and(expert_of == own_expert, count_ref[...] > low), 1.0, 0.0),
        axis=1,
        keepdims=True,
    )

    group = lax.div(lax.broadcasted_iota(jnp.int32, (1, low, 128), 2), STRIP)
    per_tile = 128 // STRIP

    def pack(m, h, store):
        units, start = UNITS[m], sum(UNITS[:m])
        tiles = 2 * nx * units * STRIP // 128

        def gathered(tile):
            out = None
            for a in range(per_tile):
                owner, strip = divmod(tile * per_tile + a, units)
                at = owner * shard + (start + strip) * STRIP
                base, off = at // 128 * 128, at % 128
                moved = scaled[h, :, :, base : base + 128]
                shift = (a * STRIP - off) % 128
                if shift:
                    moved = pltpu.roll(moved, shift, 2)
                out = moved if out is None else jnp.where(group == a, moved, out)
            return out

        for tile in range(tiles // 2):
            both = jnp.concatenate([gathered(tile), gathered(tile + tiles // 2)], axis=1)
            store(slice(tile * 128, (tile + 1) * 128), both.astype(BF16))

    def pack_both(m):
        def to_outward(at, value):
            outward[m][:, :, at] = value

        def to_own(at, value):
            halves[m][yl, :, :, at] = value

        pack(m, 1 - yl, to_outward)
        pack(m, yl, to_own)

    def y_copy(m):
        return remote(outward[m], halves[m].at[yl], ys_s.at[m], yr_s.at[m], y_pair)

    def y_arrived(m):
        remote(outward[m], halves[m].at[1 - yl], ys_s.at[m], yr_s.at[m], y_pair).wait_recv()

    def combine(m):
        span = origin[m].shape[-1]

        def join(b):
            one, two = halves[m][0, b].astype(F32), halves[m][1, b].astype(F32)
            return (
                jnp.concatenate([one[:low], two[:low]], axis=0).astype(BF16),
                jnp.concatenate([one[low:], two[low:]], axis=0).astype(BF16),
            )

        left, right = join(flight)
        for d in range(2):
            origin[m][d, 0, :, : span // 2] = left
            origin[m][d, 0, :, span // 2 :] = right
        columns[m][1, z, :, : span // 2] = left
        columns[m][1, z, :, span // 2 :] = right
        for q in range(near // 2):
            for d in range(2):
                if d == 0:
                    e = lax.rem(own_expert + near // 2 - 1 + zl - q, flight)
                else:
                    e = lax.rem(own_expert + flight - near // 2 + zl + q, flight)
                left, right = join(e)
                origin[m][d, 1 + q, :, : span // 2] = left
                origin[m][d, 1 + q, :, span // 2 :] = right
        left, right = join(own_expert)
        columns[m][0, z, :, : span // 2] = left
        columns[m][0, z, :, span // 2 :] = right

    def ring_at(m, d, k):
        at = step_start(near, k)
        return ring[m].at[d, at : at + step_size(near, k)]

    def ring_copy(m, d, k):
        size = step_size(near, k)
        src = origin[m].at[d, :size] if k == 1 else ring_at(m, d, k - 1).at[:size]
        return remote(
            src, ring_at(m, d, k), zs_s.at[m, d, k - 1], zr_s.at[m, d, k - 1], z_next[d]
        )

    def last_copy(m):
        at = step_start(near, near - 1)
        return remote(
            ring[m].at[zl, at : at + step_size(near, near)],
            last[m],
            zs_s.at[m, 0, near - 1],
            zr_s.at[m, 0, near - 1],
            z_pair,
        )

    def ring_begin(m):
        y_arrived(m)
        combine(m)
        for d in range(2):
            ring_copy(m, d, 1).start()

    def ring_step(m, k):
        if k == near:
            last_copy(m).wait_recv()
            far = lax.rem(z + near, nz)
            columns[m][0, far] = last[m][1]
            columns[m][1, far] = last[m][0]
            return
        for d in range(2):
            ring_copy(m, d, k).wait_recv()
            if k + 1 < near:
                ring_copy(m, d, k + 1).start()
        if k + 1 == near:
            last_copy(m).start()
        for d in range(2):
            source = lax.rem(z + (nz - k if d == 0 else k), nz)
            base = step_start(near, k)
            keep = base + step_size(near, k) - 1
            if k % 2 == 0:
                keep = keep - (1 - zl if d == 0 else zl)
            columns[m][0, source] = ring[m][d, keep]
            columns[m][1, source] = ring[m][d, base]

    def weights_out(yh_):
        return (
            jnp.logical_and(yh_ == yh, yl == yh),
            remote(
                wown,
                wfull.at[yl, x, c],
                ws_s.at[yh_],
                wr_s.at[yl],
                {"dp": dp_of(yh_, x), "expert": z * 2 + yh},
            ),
        )

    def weights_in(yl_):
        return remote(wown, wfull.at[yl_, x, c], ws_s.at[0], wr_s.at[yl_], y_pair)

    def weights_along(step):
        slot = wfull.at[:, x, c]
        return remote(slot, slot, ws_s.at[1 + step], wr_s.at[1 + step], x_next(step))

    def weights_along_in(step):
        slot = wfull.at[:, lax.rem(x + nx - step, nx), c]
        return remote(slot, slot, ws_s.at[1 + step], wr_s.at[1 + step], sibling)

    def weights_over(core):
        slot = wfull.at[:, :, core]
        return remote(slot, slot, ws_s.at[1 + nx], wr_s.at[1 + nx], sibling)

    def send_weights():
        loads[3].wait()
        wown[...] = master_ref[...].astype(BF16)
        for yh_ in range(2):
            own, copy = weights_out(yh_)

            @pl.when(jnp.logical_not(own))
            def _(copy=copy):
                copy.start()

            @pl.when(own)
            def _():
                pltpu.make_async_copy(wown, wfull.at[yl, x, c], wr_s.at[yl]).start()

    def pass_weights():
        for yl_ in range(2):
            weights_in(yl_).wait_recv()
        for step in range(1, nx):
            weights_along(step).start()

    def share_weights():
        for step in range(1, nx):
            weights_along_in(step).wait_recv()
        weights_over(c).start()

    def weights_sent():
        for yh_ in range(2):
            own, copy = weights_out(yh_)

            @pl.when(jnp.logical_not(own))
            def _(copy=copy):
                copy.wait_send()

        for step in range(1, nx):
            weights_along(step).wait_send()
        weights_over(c).wait_send()

    def swish(k, carry):
        at = pl.ds(pl.multiple_of(k * 2 * slots, 2 * slots), 2 * slots)
        to = pl.ds(pl.multiple_of(k * slots, slots), slots)
        gate = gate_ref[at, :].astype(F32)
        up = up_ref[at, :].astype(F32)
        value = gate * jax.nn.sigmoid(gate) * up
        hid[yl, 0, to, :] = jnp.concatenate([value[:low], value[slots : slots + low]], 0).astype(
            BF16
        )
        extra = jnp.concatenate([value[low:slots], value[slots + low :]], 0)
        hid[yl, 1, to, :] = (extra * hot).astype(BF16)
        return carry

    hid_copy = remote(hid.at[yl], hid.at[yl], pair_s.at[0], pair_s.at[1], y_pair)

    def send_hidden():
        loads[4].wait()
        loads[5].wait()
        lax.fori_loop(0, nz, swish, 0)
        hid_copy.start()

    def hidden_arrived():
        remote(hid.at[yl], hid.at[1 - yl], pair_s.at[0], pair_s.at[1], y_pair).wait_recv()

    starts = [sum(UNITS[:m]) * STRIP for m in range(chunks)]
    counts = [units * STRIP for units in UNITS]

    def to_sibling(m):
        return remote(gsend[m], grecv[m], gs_s.at[m], gr_s.at[m], sibling)

    def columns_of(m):
        return columns[m][...].reshape(2 * nz * slots, columns[m].shape[-1])

    def gradient(m):
        for y_ in range(2):
            part[m][y_] = lax.dot_general(
                columns_of(m), hid[y_].reshape(-1, cols), (((0,), (0,)), ((), ())), preferred_element_type=F32
            ).reshape(nx, 2, counts[m], cols)
        gsend[m][...] = part[m][:, :, 1 - c].astype(BF16)
        to_sibling(m).start()

    def back(m):
        for y_ in range(2):
            block = wfull[y_, :, :, starts[m] : starts[m] + counts[m], :].reshape(-1, cols)
            product = jnp.dot(columns_of(m), block, preferred_element_type=F32)
            if m:
                total[y_] += product
            else:
                total[y_] = product

    def along_copy(m, step):
        return remote(
            summed[m].at[:, lax.rem(x + step, nx)],
            across[m].at[step - 1],
            xs_s.at[m, step - 1],
            xr_s.at[m, step - 1],
            x_next(step),
        )

    def piece_copy(m, y_):
        own = jnp.logical_and(yh == yl, yl == y_)
        src, dst, sem = row_sum[m].at[y_], pieces[m].at[yh], pr_s.at[m, yh]
        to = {"dp": dp_of(yl, x), "expert": z * 2 + y_}
        return own, remote(src, dst, ps_s.at[m, y_], sem, to), (src, dst, sem)

    def reduce_cores(m):
        to_sibling(m).wait_recv()
        summed[m][...] = (part[m][:, :, c] + grecv[m][...].astype(F32)).astype(BF16)
        for step in range(1, nx):
            along_copy(m, step).start()

    def reduce_along(m):
        for step in range(1, nx):
            along_copy(m, step).wait_recv()
        value = summed[m][:, x].astype(F32)
        for step in range(1, nx):
            value += across[m][step - 1].astype(F32)
        row_sum[m][...] = value.astype(BF16)
        for y_ in range(2):
            own, copy, local = piece_copy(m, y_)

            @pl.when(jnp.logical_not(own))
            def _(copy=copy):
                copy.start()

            @pl.when(own)
            def _(local=local):
                pltpu.make_async_copy(*local).start()

    def rows_of(m):
        return pl.ds(starts[m], counts[m])

    def fresh_across(m, yh_):
        slot = fresh_ref.at[yh_, x, c, rows_of(m)]
        return remote(slot, slot, as_s.at[m, 0], ar_s.at[m, 0], y_across)

    def fresh_along(m, step, x_):
        slot = fresh_ref.at[:, x_, c, rows_of(m)]
        return remote(slot, slot, as_s.at[m, step], ar_s.at[m, step], x_next(step))

    def fresh_over(m, core):
        slot = fresh_ref.at[:, :, core, rows_of(m)]
        return remote(slot, slot, cs_s.at[m], cr_s.at[m], sibling)

    def update(m):
        for yh_ in range(2):
            remote(
                row_sum[m].at[0], pieces[m].at[yh_], ps_s.at[m, 0], pr_s.at[m, yh_], sibling
            ).wait_recv()
        at = slice(starts[m], starts[m] + counts[m])
        grad = pieces[m][0].astype(F32) + pieces[m][1].astype(F32)
        master = master_ref[at, :]
        moment_a = beta_one * first_ref[at, :] + (1.0 - beta_one) * grad
        moment_b = beta_two * second_ref[at, :] + (1.0 - beta_two) * grad * grad
        step = (
            moment_a
            / (1.0 - beta_one**5)
            / (jnp.sqrt(moment_b / (1.0 - beta_two**5)) + epsilon)
        )
        updated = master - learning_rate * (step + decay_rate * master)
        fresh_ref[yh, x, c, at, :] = updated.astype(BF16)
        fresh_across(m, yh).start()
        newm_ref[at, :] = updated
        newf_ref[at, :] = moment_a
        news_ref[at, :] = moment_b

    def gather_along(m):
        fresh_across(m, 1 - yh).wait_recv()
        for step in range(1, nx):
            fresh_along(m, step, x).start()

    def gather_over(m):
        for step in range(1, nx):
            fresh_along(m, step, lax.rem(x + nx - step, nx)).wait_recv()
        fresh_over(m, c).start()

    dh_copy = remote(dh_out, dh_in, pair_s.at[2], pair_s.at[3], y_pair)

    def finish_hidden():
        dh_copy.wait_recv()

        def one(k, carry):
            at = pl.ds(pl.multiple_of(k * 2 * slots, 2 * slots), 2 * slots)
            base = pl.ds(pl.multiple_of(k * slots, slots), slots)
            extra = pl.ds(pl.multiple_of((nz + k) * slots, slots), slots)
            gate = gate_ref[at, :].astype(F32)
            up = up_ref[at, :].astype(F32)
            sig = jax.nn.sigmoid(gate)
            low_rows = total[yl, base, :] + dh_in[base, :].astype(F32)
            high_rows = (total[yl, extra, :] + dh_in[extra, :].astype(F32)) * hot
            dh = jnp.concatenate(
                [low_rows[:low], high_rows[:low], low_rows[low:], high_rows[low:]], axis=0
            )
            dgate_ref[at, :] = (dh * up * sig * (1.0 + gate * (1.0 - sig))).astype(BF16)
            dup_ref[at, :] = (dh * (gate * sig)).astype(BF16)
            return carry

        lax.fori_loop(0, nz, one, 0)

    def products(m):
        gradient(m)
        back(m)
        if m == chunks - 1:
            dh_out[...] = total[1 - yl].astype(BF16)
            dh_copy.start()

    stages = (products, reduce_cores, reduce_along, update, gather_along, gather_over)

    def beat(tick):
        for m in range(chunks):
            stage = tick - BEGIN[m] - near
            if 0 <= stage < len(stages):
                stages[stage](m)

    pack_both(0)
    pl.semaphore_wait(barrier, nx + 5)
    y_copy(0).start()
    for m in range(1, chunks):
        pack_both(m)
        y_copy(m).start()
    for tick in range(BEGIN[-1] + near + 1):
        for m in range(chunks):
            k = tick - BEGIN[m]
            if k == 0:
                ring_begin(m)
            elif 1 <= k <= near:
                ring_step(m, k)
        if tick == 0:
            send_weights()
            send_hidden()
        if tick == 2:
            pass_weights()
        if tick == near - 2:
            share_weights()
        if tick == near:
            hidden_arrived()
            loads[6].wait()
            loads[7].wait()
            weights_over(1 - c).wait_recv()
        beat(tick)
    for m in range(chunks):
        y_copy(m).wait_send()
        for k in range(1, near):
            for d in range(2):
                ring_copy(m, d, k).wait_send()
        last_copy(m).wait_send()
    weights_sent()
    hid_copy.wait_send()
    for tick in range(BEGIN[-1] + near + 1, BEGIN[-1] + near + 6):
        beat(tick)
        if tick == BEGIN[-1] + near + 2:
            finish_hidden()
    dh_copy.wait_send()
    for m in range(chunks):
        to_sibling(m).wait_send()
        for step in range(1, nx):
            along_copy(m, step).wait_send()
        for y_ in range(2):
            own, copy, _ = piece_copy(m, y_)

            @pl.when(jnp.logical_not(own))
            def _(copy=copy):
                copy.wait_send()

        fresh_across(m, yh).wait_send()
        for step in range(1, nx):
            fresh_along(m, step, x).wait_send()
        fresh_over(m, c).wait_send()
        fresh_over(m, 1 - c).wait_recv()


def hand_over(*refs):
    count = (len(refs) - 2) // 3
    sources, results, held = (refs[k * count : (k + 1) * count] for k in range(3))
    in_s, out_s = refs[-2:]
    loads = [
        pltpu.make_async_copy(sources[k], held[k], in_s.at[k]) for k in range(count)
    ]
    stores = [
        pltpu.make_async_copy(held[k], results[k], out_s.at[k]) for k in range(count)
    ]
    for load in loads:
        load.start()
    for load, store in zip(loads, stores):
        load.wait()
        store.start()
    for store in stores:
        store.wait()


def local(nx, nz, rows, weight, count, gate, up, master, first, second):
    _, flight, slots, width = rows.shape
    shard, cols = master.shape
    _, received, _ = gate.shape
    chunks = len(UNITS)
    counts = [units * STRIP for units in UNITS]
    assert sum(counts) == shard and cols % 128 == 0
    spans = [2 * nx * n for n in counts]
    vmem = pl.BlockSpec(memory_space=pltpu.VMEM)
    dma = pltpu.SemaphoreType.DMA
    near = nz // 2
    blocks = step_start(near, near)
    hbm = pl.BlockSpec(memory_space=pltpu.HBM)
    scratch = (
        [pltpu.VMEM((flight + 1, slots, n // 2), BF16) for n in spans]
        + [pltpu.VMEM((2, flight + 1, slots, n // 2), BF16) for n in spans]
        + [pltpu.VMEM((2, near // 2 + 1, slots, n), BF16) for n in spans]
        + [pltpu.VMEM((2, blocks, slots, n), BF16) for n in spans]
        + [pltpu.VMEM((step_size(near, near), slots, n), BF16) for n in spans]
        + [pltpu.VMEM((2, nz, slots, n), BF16) for n in spans]
        + [pltpu.VMEM((2, nx, 2, n, cols), F32) for n in counts]
        + [pltpu.VMEM((2, nx, n, cols), BF16) for n in counts]
        + [pltpu.VMEM((2, nx, n, cols), BF16) for n in counts]
        + [pltpu.VMEM((2, nx, n, cols), BF16) for n in counts]
        + [pltpu.VMEM((nx - 1, 2, n, cols), BF16) for n in counts]
        + [pltpu.VMEM((2, n, cols), BF16) for n in counts]
        + [pltpu.VMEM((2, n, cols), BF16) for n in counts]
        + [
            pltpu.VMEM((flight, slots, width), BF16),
            pltpu.VMEM((flight, slots), F32),
            pltpu.VMEM((1, flight), jnp.int32),
            pltpu.VMEM((received, cols), BF16),
            pltpu.VMEM((received, cols), BF16),
            pltpu.VMEM((shard, cols), F32),
            pltpu.VMEM((shard, cols), F32),
            pltpu.VMEM((shard, cols), F32),
            dma((8,)),
            pltpu.VMEM((2, flight + 1, slots // 2, width // 2), F32),
            pltpu.VMEM((shard, cols), BF16),
            pltpu.VMEM((2, nx, 2, shard, cols), BF16),
            pltpu.VMEM((2, 2, received // 2, cols), BF16),
            pltpu.VMEM((2, received, cols), F32),
            pltpu.VMEM((received, cols), BF16),
            pltpu.VMEM((received, cols), BF16),
            dma((chunks,)),
            dma((chunks,)),
            dma((chunks, 2, near)),
            dma((chunks, 2, near)),
            dma((nx + 2,)),
            dma((nx + 2,)),
            dma((4,)),
            dma((chunks,)),
            dma((chunks,)),
            dma((chunks, nx - 1)),
            dma((chunks, nx - 1)),
            dma((chunks, 2)),
            dma((chunks, 2)),
            dma((chunks, nx)),
            dma((chunks, nx)),
            dma((chunks,)),
            dma((chunks,)),
        ]
    )
    outs = pl.pallas_call(
        functools.partial(kernel, nx, nz),
        out_shape=[
            jax.ShapeDtypeStruct((received, cols), BF16),
            jax.ShapeDtypeStruct((received, cols), BF16),
            jax.ShapeDtypeStruct((shard, cols), F32),
            jax.ShapeDtypeStruct((shard, cols), F32),
            jax.ShapeDtypeStruct((shard, cols), F32),
            jax.ShapeDtypeStruct((2, nx, 2, shard, cols), BF16),
        ],
        in_specs=[hbm] * 8,
        out_specs=[vmem] * 6,
        scratch_shapes=scratch,
        compiler_params=pltpu.CompilerParams(
            collective_id=0, has_side_effects=True, vmem_limit_bytes=62 * 1024 * 1024
        ),
    )(rows[0], weight[0], count, gate[0], up[0], master, first, second)
    outs = pl.pallas_call(
        hand_over,
        out_shape=[jax.ShapeDtypeStruct(o.shape, o.dtype) for o in outs],
        in_specs=[hbm] * 6,
        out_specs=[hbm] * 6,
        scratch_shapes=[pltpu.VMEM(o.shape, o.dtype) for o in outs] + [dma((6,)), dma((6,))],
        compiler_params=pltpu.CompilerParams(vmem_limit_bytes=62 * 1024 * 1024),
    )(*outs)
    return (
        outs[0][None],
        outs[1][None],
        outs[2],
        outs[3],
        outs[4],
        outs[5].reshape(4 * nx * shard, cols),
    )


def solution(mesh):
    nx, nz = mesh.shape["dp"] // 4, mesh.shape["expert"] // 2
    placed = (
        P("dp", "expert", None, None),
        P("dp", "expert", None),
        P("dp", "expert"),
        P("dp", None, "expert"),
        P("dp", None, "expert"),
        P("dp", "expert"),
        P("dp", "expert"),
        P("dp", "expert"),
    )
    return jax.shard_map(
        functools.partial(local, nx, nz),
        mesh=mesh,
        in_specs=placed,
        out_specs=(
            P("dp", None, "expert"),
            P("dp", None, "expert"),
            P("dp", "expert"),
            P("dp", "expert"),
            P("dp", "expert"),
            P(None, "expert"),
        ),
        check_vma=False,
    )
```

```python
import functools

import jax
import jax.numpy as jnp
from jax import lax
from jax.experimental import pallas as pl
from jax.experimental.pallas import tpu as pltpu
from jax.sharding import PartitionSpec as P

UNITS = (2, 2, 2, 1)
STRIP = 32

learning_rate = 0.01
beta_one = 0.9
beta_two = 0.95
decay_rate = 0.1
epsilon = 1e-08

MESH = pl.DeviceIdType.MESH
BF16 = jnp.bfloat16
F32 = jnp.float32


def step_size(near, k):
    return (near - k) // 2 + 2


def step_start(near, k):
    return sum(step_size(near, j) for j in range(1, k))


def kernel(
    nx,
    nz,
    rows_hbm,
    weight_hbm,
    count_hbm,
    gate_hbm,
    up_hbm,
    master_hbm,
    first_hbm,
    second_hbm,
    dgate_ref,
    dup_ref,
    newm_ref,
    newf_ref,
    news_ref,
    fresh_ref,
    *scratch,
):
    chunks = len(UNITS)
    (
        outward,
        halves,
        origin,
        ring,
        last,
        columns,
        part,
        gsend,
        grecv,
        summed,
        across,
        row_sum,
        pieces,
    ) = (scratch[k * chunks : (k + 1) * chunks] for k in range(13))
    (
        rows_ref,
        weight_ref,
        count_ref,
        gate_ref,
        up_ref,
        master_ref,
        first_ref,
        second_ref,
        in_s,
        scaled,
        wown,
        wfull,
        hid,
        total,
        dh_out,
        dh_in,
        ys_s,
        yr_s,
        zs_s,
        zr_s,
        ws_s,
        wr_s,
        pair_s,
        gs_s,
        gr_s,
        xs_s,
        xr_s,
        ps_s,
        pr_s,
        as_s,
        ar_s,
        cs_s,
        cr_s,
    ) = scratch[13 * chunks :]
    flight, slots, width = rows_ref.shape
    shard, cols = master_ref.shape
    half = width // 2
    near = nz // 2
    low = slots // 2

    i, ez = lax.axis_index("dp"), lax.axis_index("expert")
    c, x, yh = lax.rem(i, 2), lax.rem(lax.div(i, 2), nx), lax.div(i, 2 * nx)
    z, yl = lax.div(ez, 2), lax.rem(ez, 2)
    zl, own_expert = lax.rem(z, 2), lax.div(z, 2)
    sibling = {"dp": i + 1 - 2 * c}
    z_pair = {"expert": ez + 2 - 4 * zl}
    y_pair = {"expert": ez + 1 - 2 * yl}
    y_across = {"dp": i + (1 - 2 * yh) * 2 * nx}
    z_next = (
        {"expert": lax.rem(z + 1, nz) * 2 + yl},
        {"expert": lax.rem(z + nz - 1, nz) * 2 + yl},
    )

    def dp_of(yh_, x_):
        return yh_ * (2 * nx) + x_ * 2 + c

    def x_next(step):
        return {"dp": dp_of(yh, lax.rem(x + step, nx))}

    def remote(src, dst, s, r, to):
        return pltpu.make_async_remote_copy(
            src_ref=src, dst_ref=dst, send_sem=s, recv_sem=r, device_id=to, device_id_type=MESH
        )

    loads = [
        pltpu.make_async_copy(src, dst, in_s.at[k])
        for k, (src, dst) in enumerate(
            (
                (rows_hbm, rows_ref),
                (weight_hbm, weight_ref),
                (count_hbm, count_ref),
                (master_hbm, master_ref),
                (gate_hbm, gate_ref),
                (up_hbm, up_ref),
                (first_hbm, first_ref),
                (second_hbm, second_ref),
            )
        )
    ]
    for load in loads:
        load.start()

    barrier = pltpu.get_barrier_semaphore()

    def greet(to):
        pl.semaphore_signal(barrier, inc=1, device_id=to, device_id_type=MESH)

    greet(z_next[0])
    greet(z_next[1])
    greet(sibling)

    greet(y_pair)
    greet(y_across)
    greet({"dp": dp_of(1 - yh, x), "expert": ez + 1 - 2 * yl})
    for step in range(1, nx):
        greet(x_next(step))

    for load in loads[:3]:
        load.wait()
    eye = lax.broadcasted_iota(jnp.int32, (slots, slots), 0) == lax.broadcasted_iota(
        jnp.int32, (slots, slots), 1
    )
    slot_of = lax.broadcasted_iota(jnp.int32, (slots, 1), 0)
    for e in range(flight):
        factor = jnp.sum(
            jnp.where(eye, jnp.broadcast_to(weight_ref[e : e + 1, :], (slots, slots)), 0.0),
            axis=1,
            keepdims=True,
        )
        factor = jnp.where(slot_of < count_ref[:, e : e + 1], factor, 0.0)
        block = rows_ref[e].astype(F32) * factor
        for h in range(2):
            side = block[:, h * half : (h + 1) * half]
            scaled[h, e] = side[:low]
            if e:
                scaled[h, flight] += side[low:]
            else:
                scaled[h, flight] = side[low:]
    expert_of = lax.broadcasted_iota(jnp.int32, (1, flight), 1)
    hot = jnp.max(
        jnp.where(jnp.logical_and(expert_of == own_expert, count_ref[...] > low), 1.0, 0.0),
        axis=1,
        keepdims=True,
    )

    group = lax.div(lax.broadcasted_iota(jnp.int32, (1, low, 128), 2), STRIP)
    per_tile = 128 // STRIP

    def pack(m, h, store):
        units, start = UNITS[m], sum(UNITS[:m])
        tiles = 2 * nx * units * STRIP // 128

        def gathered(tile):
            out = None
            for a in range(per_tile):
                owner, strip = divmod(tile * per_tile + a, units)
                at = owner * shard + (start + strip) * STRIP
                base, off = at // 128 * 128, at % 128
                moved = scaled[h, :, :, base : base + 128]
                shift = (a * STRIP - off) % 128
                if shift:
                    moved = pltpu.roll(moved, shift, 2)
                out = moved if out is None else jnp.where(group == a, moved, out)
            return out

        for tile in range(tiles // 2):
            both = jnp.concatenate([gathered(tile), gathered(tile + tiles // 2)], axis=1)
            store(slice(tile * 128, (tile + 1) * 128), both.astype(BF16))

    def pack_outward(m):
        def store(at, value):
            outward[m][:, :, at] = value

        pack(m, 1 - yl, store)

    def pack_own(m):
        def store(at, value):
            halves[m][yl, :, :, at] = value

        pack(m, yl, store)

    def y_copy(m):
        return remote(outward[m], halves[m].at[yl], ys_s.at[m], yr_s.at[m], y_pair)

    def y_arrived(m):
        remote(outward[m], halves[m].at[1 - yl], ys_s.at[m], yr_s.at[m], y_pair).wait_recv()

    def join(m, b):
        one, two = halves[m][0, b].astype(F32), halves[m][1, b].astype(F32)
        return (
            jnp.concatenate([one[:low], two[:low]], axis=0).astype(BF16),
            jnp.concatenate([one[low:], two[low:]], axis=0).astype(BF16),
        )

    def combine(m, d):
        span = origin[m].shape[-1]
        left, right = join(m, flight)
        origin[m][d, 0, :, : span // 2] = left
        origin[m][d, 0, :, span // 2 :] = right
        for q in range(near // 2):
            if d == 0:
                e = lax.rem(own_expert + near // 2 - 1 + zl - q, flight)
            else:
                e = lax.rem(own_expert + flight - near // 2 + zl + q, flight)
            left, right = join(m, e)
            origin[m][d, 1 + q, :, : span // 2] = left
            origin[m][d, 1 + q, :, span // 2 :] = right

    def keep_own(m):
        columns[m][0, z] = origin[m][zl, near // 2]
        columns[m][1, z] = origin[m][0, 0]

    def ring_at(m, d, k):
        at = step_start(near, k)
        return ring[m].at[d, at : at + step_size(near, k)]

    def ring_copy(m, d, k):
        size = step_size(near, k)
        src = origin[m].at[d, :size] if k == 1 else ring_at(m, d, k - 1).at[:size]
        return remote(
            src, ring_at(m, d, k), zs_s.at[m, d, k - 1], zr_s.at[m, d, k - 1], z_next[d]
        )

    def last_copy(m):
        at = step_start(near, near - 1)
        return remote(
            ring[m].at[zl, at : at + step_size(near, near)],
            last[m],
            zs_s.at[m, 0, near - 1],
            zr_s.at[m, 0, near - 1],
            z_pair,
        )

    def ring_begin(m):
        y_arrived(m)
        for d in range(2):
            combine(m, d)
            ring_copy(m, d, 1).start()

    def ring_pass(m, k):
        if k == near:
            last_copy(m).wait_recv()
            return
        for d in range(2):
            ring_copy(m, d, k).wait_recv()
            if k + 1 < near:
                ring_copy(m, d, k + 1).start()
        if k + 1 == near:
            last_copy(m).start()

    def ring_keep(m, k):
        if k == near:
            far = lax.rem(z + near, nz)
            columns[m][0, far] = last[m][1]
            columns[m][1, far] = last[m][0]
            return
        for d in range(2):
            source = lax.rem(z + (nz - k if d == 0 else k), nz)
            base = step_start(near, k)
            keep = base + step_size(near, k) - 1
            if k % 2 == 0:
                keep = keep - (1 - zl if d == 0 else zl)
            columns[m][0, source] = ring[m][d, keep]
            columns[m][1, source] = ring[m][d, base]

    def weights_out(yh_):
        return (
            jnp.logical_and(yh_ == yh, yl == yh),
            remote(
                wown,
                wfull.at[yl, x, c],
                ws_s.at[yh_],
                wr_s.at[yl],
                {"dp": dp_of(yh_, x), "expert": z * 2 + yh},
            ),
        )

    def weights_in(yl_):
        return remote(wown, wfull.at[yl_, x, c], ws_s.at[0], wr_s.at[yl_], y_pair)

    def weights_along(step):
        slot = wfull.at[:, x, c]
        return remote(slot, slot, ws_s.at[1 + step], wr_s.at[1 + step], x_next(step))

    def weights_along_in(step):
        slot = wfull.at[:, lax.rem(x + nx - step, nx), c]
        return remote(slot, slot, ws_s.at[1 + step], wr_s.at[1 + step], sibling)

    def weights_over(core):
        slot = wfull.at[:, :, core]
        return remote(slot, slot, ws_s.at[1 + nx], wr_s.at[1 + nx], sibling)

    def send_weights():
        loads[3].wait()
        wown[...] = master_ref[...].astype(BF16)
        for yh_ in range(2):
            own, copy = weights_out(yh_)

            @pl.when(jnp.logical_not(own))
            def _(copy=copy):
                copy.start()

            @pl.when(own)
            def _():
                pltpu.make_async_copy(wown, wfull.at[yl, x, c], wr_s.at[yl]).start()

    def pass_weights():
        for yl_ in range(2):
            weights_in(yl_).wait_recv()
        for step in range(1, nx):
            weights_along(step).start()

    def share_weights():
        for step in range(1, nx):
            weights_along_in(step).wait_recv()
        weights_over(c).start()

    def weights_sent():
        for yh_ in range(2):
            own, copy = weights_out(yh_)

            @pl.when(jnp.logical_not(own))
            def _(copy=copy):
                copy.wait_send()

        for step in range(1, nx):
            weights_along(step).wait_send()
        weights_over(c).wait_send()

    def swish(k, carry):
        at = pl.ds(pl.multiple_of(k * 2 * slots, 2 * slots), 2 * slots)
        to = pl.ds(pl.multiple_of(k * slots, slots), slots)
        gate = gate_ref[at, :].astype(F32)
        up = up_ref[at, :].astype(F32)
        value = gate * jax.nn.sigmoid(gate) * up
        hid[yl, 0, to, :] = jnp.concatenate([value[:low], value[slots : slots + low]], 0).astype(
            BF16
        )
        extra = jnp.concatenate([value[low:slots], value[slots + low :]], 0)
        hid[yl, 1, to, :] = (extra * hot).astype(BF16)
        return carry

    hid_copy = remote(hid.at[yl], hid.at[yl], pair_s.at[0], pair_s.at[1], y_pair)

    def send_hidden():
        loads[4].wait()
        loads[5].wait()
        lax.fori_loop(0, nz, swish, 0)
        hid_copy.start()

    def hidden_arrived():
        remote(hid.at[yl], hid.at[1 - yl], pair_s.at[0], pair_s.at[1], y_pair).wait_recv()

    starts = [sum(UNITS[:m]) * STRIP for m in range(chunks)]
    counts = [units * STRIP for units in UNITS]

    def to_sibling(m):
        return remote(gsend[m], grecv[m], gs_s.at[m], gr_s.at[m], sibling)

    def columns_of(m):
        return columns[m][...].reshape(2 * nz * slots, columns[m].shape[-1])

    def gradient(m):
        for y_ in range(2):
            part[m][y_] = lax.dot_general(
                columns_of(m), hid[y_].reshape(-1, cols), (((0,), (0,)), ((), ())), preferred_element_type=F32
            ).reshape(nx, 2, counts[m], cols)
        gsend[m][...] = part[m][:, :, 1 - c].astype(BF16)
        to_sibling(m).start()

    def back(m):
        for y_ in range(2):
            block = wfull[y_, :, :, starts[m] : starts[m] + counts[m], :].reshape(-1, cols)
            product = jnp.dot(columns_of(m), block, preferred_element_type=F32)
            if m:
                total[y_] += product
            else:
                total[y_] = product

    def along_copy(m, step):
        return remote(
            summed[m].at[:, lax.rem(x + step, nx)],
            across[m].at[step - 1],
            xs_s.at[m, step - 1],
            xr_s.at[m, step - 1],
            x_next(step),
        )

    def piece_copy(m, y_):
        own = jnp.logical_and(yh == yl, yl == y_)
        src, dst, sem = row_sum[m].at[y_], pieces[m].at[yh], pr_s.at[m, yh]
        to = {"dp": dp_of(yl, x), "expert": z * 2 + y_}
        return own, remote(src, dst, ps_s.at[m, y_], sem, to), (src, dst, sem)

    def reduce_cores(m):
        to_sibling(m).wait_recv()
        summed[m][...] = (part[m][:, :, c] + grecv[m][...].astype(F32)).astype(BF16)
        for step in range(1, nx):
            along_copy(m, step).start()

    def reduce_along(m):
        for step in range(1, nx):
            along_copy(m, step).wait_recv()
        value = summed[m][:, x].astype(F32)
        for step in range(1, nx):
            value += across[m][step - 1].astype(F32)
        row_sum[m][...] = value.astype(BF16)
        for y_ in range(2):
            own, copy, local = piece_copy(m, y_)

            @pl.when(jnp.logical_not(own))
            def _(copy=copy):
                copy.start()

            @pl.when(own)
            def _(local=local):
                pltpu.make_async_copy(*local).start()

    def rows_of(m):
        return pl.ds(starts[m], counts[m])

    def fresh_across(m, yh_):
        slot = fresh_ref.at[yh_, x, c, rows_of(m)]
        return remote(slot, slot, as_s.at[m, 0], ar_s.at[m, 0], y_across)

    def fresh_along(m, step, x_):
        slot = fresh_ref.at[:, x_, c, rows_of(m)]
        return remote(slot, slot, as_s.at[m, step], ar_s.at[m, step], x_next(step))

    def fresh_over(m, core):
        slot = fresh_ref.at[:, :, core, rows_of(m)]
        return remote(slot, slot, cs_s.at[m], cr_s.at[m], sibling)

    def update(m):
        for yh_ in range(2):
            remote(
                row_sum[m].at[0], pieces[m].at[yh_], ps_s.at[m, 0], pr_s.at[m, yh_], sibling
            ).wait_recv()
        at = slice(starts[m], starts[m] + counts[m])
        grad = pieces[m][0].astype(F32) + pieces[m][1].astype(F32)
        master = master_ref[at, :]
        moment_a = beta_one * first_ref[at, :] + (1.0 - beta_one) * grad
        moment_b = beta_two * second_ref[at, :] + (1.0 - beta_two) * grad * grad
        step = (
            moment_a
            / (1.0 - beta_one**5)
            / (jnp.sqrt(moment_b / (1.0 - beta_two**5)) + epsilon)
        )
        updated = master - learning_rate * (step + decay_rate * master)
        fresh_ref[yh, x, c, at, :] = updated.astype(BF16)
        fresh_across(m, yh).start()
        newm_ref[at, :] = updated
        newf_ref[at, :] = moment_a
        news_ref[at, :] = moment_b

    def gather_along(m):
        fresh_across(m, 1 - yh).wait_recv()
        for step in range(1, nx):
            fresh_along(m, step, x).start()

    def gather_over(m):
        for step in range(1, nx):
            fresh_along(m, step, lax.rem(x + nx - step, nx)).wait_recv()
        fresh_over(m, c).start()

    dh_copy = remote(dh_out, dh_in, pair_s.at[2], pair_s.at[3], y_pair)

    def finish_hidden():
        dh_copy.wait_recv()

        def one(k, carry):
            at = pl.ds(pl.multiple_of(k * 2 * slots, 2 * slots), 2 * slots)
            base = pl.ds(pl.multiple_of(k * slots, slots), slots)
            extra = pl.ds(pl.multiple_of((nz + k) * slots, slots), slots)
            gate = gate_ref[at, :].astype(F32)
            up = up_ref[at, :].astype(F32)
            sig = jax.nn.sigmoid(gate)
            low_rows = total[yl, base, :] + dh_in[base, :].astype(F32)
            high_rows = (total[yl, extra, :] + dh_in[extra, :].astype(F32)) * hot
            dh = jnp.concatenate(
                [low_rows[:low], high_rows[:low], low_rows[low:], high_rows[low:]], axis=0
            )
            dgate_ref[at, :] = (dh * up * sig * (1.0 + gate * (1.0 - sig))).astype(BF16)
            dup_ref[at, :] = (dh * (gate * sig)).astype(BF16)
            return carry

        lax.fori_loop(0, nz, one, 0)

    def products(m):
        gradient(m)
        back(m)
        if m == chunks - 1:
            dh_out[...] = total[1 - yl].astype(BF16)
            dh_copy.start()

    expected = (
        (reduce_cores, 3.0, 0.3),
        (reduce_along, 9.2, 2.7),
        (update, 13.7, 2.7),
        (gather_along, 17.7, 2.7),
        (gather_over, 24.0, 3.0),
    )
    order = sorted(
        (first + lag * m, at, m)
        for at, (_, first, lag) in enumerate(expected)
        for m in range(chunks)
    )

    pack_outward(0)
    pl.semaphore_wait(barrier, nx + 5)
    y_copy(0).start()
    for m in range(1, chunks):
        pack_outward(m)
        y_copy(m).start()
    for m in range(chunks):
        pack_own(m)
        ring_begin(m)
    for tick in range(near):
        if tick:
            for m in range(chunks):
                ring_pass(m, tick)
            for m in range(chunks):
                ring_keep(m, tick)
        else:
            for m in range(chunks):
                keep_own(m)
        if tick == 0:
            send_weights()
            send_hidden()
        if tick == 2:
            pass_weights()
        if tick == near - 2:
            share_weights()
        if tick == near - 1:
            hidden_arrived()
            loads[6].wait()
            loads[7].wait()
            weights_over(1 - c).wait_recv()
    for m in range(chunks):
        ring_pass(m, near)
        ring_keep(m, near)
        products(m)
    hidden_done = False
    for when, at, m in order:
        if when > 16.2 and not hidden_done:
            finish_hidden()
            hidden_done = True
        expected[at][0](m)
    for m in range(chunks):
        y_copy(m).wait_send()
        for k in range(1, near):
            for d in range(2):
                ring_copy(m, d, k).wait_send()
        last_copy(m).wait_send()
    weights_sent()
    hid_copy.wait_send()
    dh_copy.wait_send()
    for m in range(chunks):
        to_sibling(m).wait_send()
        for step in range(1, nx):
            along_copy(m, step).wait_send()
        for y_ in range(2):
            own, copy, _ = piece_copy(m, y_)

            @pl.when(jnp.logical_not(own))
            def _(copy=copy):
                copy.wait_send()

        fresh_across(m, yh).wait_send()
        for step in range(1, nx):
            fresh_along(m, step, x).wait_send()
        fresh_over(m, c).wait_send()
        fresh_over(m, 1 - c).wait_recv()


def hand_over(*refs):
    count = (len(refs) - 2) // 3
    sources, results, held = (refs[k * count : (k + 1) * count] for k in range(3))
    in_s, out_s = refs[-2:]
    loads = [
        pltpu.make_async_copy(sources[k], held[k], in_s.at[k]) for k in range(count)
    ]
    stores = [
        pltpu.make_async_copy(held[k], results[k], out_s.at[k]) for k in range(count)
    ]
    for load in loads:
        load.start()
    for load, store in zip(loads, stores):
        load.wait()
        store.start()
    for store in stores:
        store.wait()


def local(nx, nz, rows, weight, count, gate, up, master, first, second):
    _, flight, slots, width = rows.shape
    shard, cols = master.shape
    _, received, _ = gate.shape
    chunks = len(UNITS)
    counts = [units * STRIP for units in UNITS]
    assert sum(counts) == shard and cols % 128 == 0
    spans = [2 * nx * n for n in counts]
    vmem = pl.BlockSpec(memory_space=pltpu.VMEM)
    dma = pltpu.SemaphoreType.DMA
    near = nz // 2
    blocks = step_start(near, near)
    hbm = pl.BlockSpec(memory_space=pltpu.HBM)
    scratch = (
        [pltpu.VMEM((flight + 1, slots, n // 2), BF16) for n in spans]
        + [pltpu.VMEM((2, flight + 1, slots, n // 2), BF16) for n in spans]
        + [pltpu.VMEM((2, near // 2 + 1, slots, n), BF16) for n in spans]
        + [pltpu.VMEM((2, blocks, slots, n), BF16) for n in spans]
        + [pltpu.VMEM((step_size(near, near), slots, n), BF16) for n in spans]
        + [pltpu.VMEM((2, nz, slots, n), BF16) for n in spans]
        + [pltpu.VMEM((2, nx, 2, n, cols), F32) for n in counts]
        + [pltpu.VMEM((2, nx, n, cols), BF16) for n in counts]
        + [pltpu.VMEM((2, nx, n, cols), BF16) for n in counts]
        + [pltpu.VMEM((2, nx, n, cols), BF16) for n in counts]
        + [pltpu.VMEM((nx - 1, 2, n, cols), BF16) for n in counts]
        + [pltpu.VMEM((2, n, cols), BF16) for n in counts]
        + [pltpu.VMEM((2, n, cols), BF16) for n in counts]
        + [
            pltpu.VMEM((flight, slots, width), BF16),
            pltpu.VMEM((flight, slots), F32),
            pltpu.VMEM((1, flight), jnp.int32),
            pltpu.VMEM((received, cols), BF16),
            pltpu.VMEM((received, cols), BF16),
            pltpu.VMEM((shard, cols), F32),
            pltpu.VMEM((shard, cols), F32),
            pltpu.VMEM((shard, cols), F32),
            dma((8,)),
            pltpu.VMEM((2, flight + 1, slots // 2, width // 2), F32),
            pltpu.VMEM((shard, cols), BF16),
            pltpu.VMEM((2, nx, 2, shard, cols), BF16),
            pltpu.VMEM((2, 2, received // 2, cols), BF16),
            pltpu.VMEM((2, received, cols), F32),
            pltpu.VMEM((received, cols), BF16),
            pltpu.VMEM((received, cols), BF16),
            dma((chunks,)),
            dma((chunks,)),
            dma((chunks, 2, near)),
            dma((chunks, 2, near)),
            dma((nx + 2,)),
            dma((nx + 2,)),
            dma((4,)),
            dma((chunks,)),
            dma((chunks,)),
            dma((chunks, nx - 1)),
            dma((chunks, nx - 1)),
            dma((chunks, 2)),
            dma((chunks, 2)),
            dma((chunks, nx)),
            dma((chunks, nx)),
            dma((chunks,)),
            dma((chunks,)),
        ]
    )
    outs = pl.pallas_call(
        functools.partial(kernel, nx, nz),
        out_shape=[
            jax.ShapeDtypeStruct((received, cols), BF16),
            jax.ShapeDtypeStruct((received, cols), BF16),
            jax.ShapeDtypeStruct((shard, cols), F32),
            jax.ShapeDtypeStruct((shard, cols), F32),
            jax.ShapeDtypeStruct((shard, cols), F32),
            jax.ShapeDtypeStruct((2, nx, 2, shard, cols), BF16),
        ],
        in_specs=[hbm] * 8,
        out_specs=[vmem] * 6,
        scratch_shapes=scratch,
        compiler_params=pltpu.CompilerParams(
            collective_id=0, has_side_effects=True, vmem_limit_bytes=62 * 1024 * 1024
        ),
    )(rows[0], weight[0], count, gate[0], up[0], master, first, second)
    outs = pl.pallas_call(
        hand_over,
        out_shape=[jax.ShapeDtypeStruct(o.shape, o.dtype) for o in outs],
        in_specs=[hbm] * 6,
        out_specs=[hbm] * 6,
        scratch_shapes=[pltpu.VMEM(o.shape, o.dtype) for o in outs] + [dma((6,)), dma((6,))],
        compiler_params=pltpu.CompilerParams(vmem_limit_bytes=62 * 1024 * 1024),
    )(*outs)
    return (
        outs[0][None],
        outs[1][None],
        outs[2],
        outs[3],
        outs[4],
        outs[5].reshape(4 * nx * shard, cols),
    )


def solution(mesh):
    nx, nz = mesh.shape["dp"] // 4, mesh.shape["expert"] // 2
    placed = (
        P("dp", "expert", None, None),
        P("dp", "expert", None),
        P("dp", "expert"),
        P("dp", None, "expert"),
        P("dp", None, "expert"),
        P("dp", "expert"),
        P("dp", "expert"),
        P("dp", "expert"),
    )
    return jax.shard_map(
        functools.partial(local, nx, nz),
        mesh=mesh,
        in_specs=placed,
        out_specs=(
            P("dp", None, "expert"),
            P("dp", None, "expert"),
            P("dp", "expert"),
            P("dp", "expert"),
            P("dp", "expert"),
            P(None, "expert"),
        ),
        check_vma=False,
    )
```
